32 devices in a mesh: seq: 8 (over y, x, core), row: 4 (over z).
Axes of the slice: x: 2, y: 2, z: 4, core: 2. Of those that a mesh axis runs over, the one named last changes fastest.
Arguments:
- tokens: bfloat16 [4, 1024, 2048], P('row', 'seq'), may hold values from -6 to 6
- cotangent: bfloat16 [4, 1024, 2048], P('row', 'seq'), may hold values from -6 to 6
- starts: int32 [4, 8], P('row'), may hold values from 0 to 1023, as said below
- gains: float32 [5120], P(('seq', 'row')), may hold values from 0.5 to 1.5
- gain_moment: float32 [5120], P(('seq', 'row')), may hold values from -40 to 40
- master_qa: float32 [2048, 1024], P(('seq', 'row')), may hold values from -0.125 to 0.125
- master_qb: float32 [1024, 4096], P(('seq', 'row')), may hold values from -0.1875 to 0.1875
- master_kv: float32 [2048, 512], P(('seq', 'row')), may hold values from -0.125 to 0.125
- master_out: float32 [4096, 2048], P(('seq', 'row')), may hold values from -1.5 to 1.5
- master_gu: float32 [2048, 11264], P(('seq', 'row')), may hold values from -0.125 to 0.125
- master_down: float32 [5632, 2048], P(('seq', 'row')), may hold values from -0.078125 to 0.078125
- left_stat: float32 [6144, 64, 64], P(('seq', 'row')), as said below
- right_stat: float32 [6144, 128, 128], P(('seq', 'row')), as said below
- left_root: float32 [6144, 64, 64], P(('seq', 'row')), as said below
- right_root: float32 [6144, 128, 128], P(('seq', 'row')), as said below
Outputs:
- output: bfloat16 [4, 1024, 2048], P('row', 'seq')
- grad_tokens: float32 [4, 1024, 2048], P('row', 'seq')
- grad_qa: float32 [2048, 1024], P(('seq', 'row'))
- grad_qb: float32 [1024, 4096], P(('seq', 'row'))
- grad_kv: float32 [2048, 512], P(('seq', 'row'))
- grad_out: float32 [4096, 2048], P(('seq', 'row'))
- grad_gu: float32 [2048, 11264], P(('seq', 'row'))
- grad_down: float32 [5632, 2048], P(('seq', 'row'))
- new_qa: float32 [2048, 1024], P(('seq', 'row'))
- new_qb: float32 [1024, 4096], P(('seq', 'row'))
- new_kv: float32 [2048, 512], P(('seq', 'row'))
- new_out: float32 [4096, 2048], P(('seq', 'row'))
- new_gu: float32 [2048, 11264], P(('seq', 'row'))
- new_down: float32 [5632, 2048], P(('seq', 'row'))
- moment_new: float32 [5120], P(('seq', 'row'))
- gains_new: float32 [5120], P(('seq', 'row'))
- left_new: float32 [6144, 64, 64], P(('seq', 'row'))
- right_new: float32 [6144, 128, 128], P(('seq', 'row'))
The draws below stay inside these ranges and needn't reach their ends.
Inputs may be any that keep to these rules, and one draw needn't show every extreme that they name: Each row's starts begin at 0 and rise strictly; the last document of each row is its last position alone. In each row one document, which one drawn per row, begins before position 128 and ends after position 896. `left_stat`: each block is symmetric, with a positive diagonal larger than the sum of magnitudes of its row's other entries. `right_stat`: each block is symmetric, with a positive diagonal larger than the sum of magnitudes of its row's other entries. `left_root`: each block is symmetric, with a positive diagonal larger than the sum of magnitudes of its row's other entries. `right_root`: each block is symmetric, with a positive diagonal larger than the sum of magnitudes of its row's other entries.
All inputs are finite; a program needn't handle non-finite values.
Results may differ from the reference program's by a relative error of at most 0.015.
The reference program's roundings to bfloat16 on the way count: a program that leaves them out, or rounds other values in their place, can miss the bound.
Values may be sent and summed in bfloat16 or wider, within the bound.
No kernel may reach another device: no remote copies, remote signals or barrier semaphores. Data moves between devices by JAX's collectives and lax.ppermute only.
A program may use at most 704 MiB of HBM per device.

```python
import math
import jax
import jax.numpy as jnp
from jax import lax

D = 2048
QR = 1024
HQ = 16
HD = 256
FF = 5632
TOK_DEV = 128
NSEG = 8
BL = 64
BC = 128
LEN = 1024
ROWS = 4
TOKENS = 4096
OWN = 32
GLEN = 5120
BPD = 192
NBLK = 6144


def block_scale(extent):
    factors = ((D * QR, 1.0), (QR * HQ * HD, 0.7), (2 * D * HD, 2.0), (HQ * HD * D, 2.0 / math.sqrt(LEN)), (2 * D * FF, 0.35), (FF * D, 0.6))
    parts_list = [jnp.full((entries // (OWN * BL * BC),), factor * factor * TOKENS * extent, jnp.float32) for entries, factor in factors]
    return jnp.tile(jnp.concatenate(parts_list), OWN)


def dominant(key, blocks, extent, scaling):
    diagonal = jnp.exp(jax.random.uniform(jax.random.fold_in(key, 1), (blocks, extent), jnp.float32, 0.0, math.log(4.0)))
    noise = jax.random.uniform(jax.random.fold_in(key, 2), (blocks, extent, extent), jnp.float32, -0.95, 0.95)
    upper_part = jnp.triu(noise, 1) / extent
    identity = jnp.eye(extent, dtype=jnp.float32)[None]
    whole = upper_part + jnp.swapaxes(upper_part, 1, 2) + diagonal[:, :, None] * identity
    return whole * scaling[:, None, None]


def draw_starts(key, part):
    key = jax.random.fold_in(key, 11)
    short_most = max(1, TOK_DEV // NSEG)
    long_index = jax.random.randint(jax.random.fold_in(key, 1), (ROWS, 1), 0, NSEG - 1)
    lengths = jax.random.randint(jax.random.fold_in(key, 2), (ROWS, NSEG), 1, short_most + 1)
    slot_index = jnp.arange(NSEG, dtype=jnp.int32)[None, :]
    lengths = jnp.where(slot_index == NSEG - 1, 1, lengths)
    before = jnp.where(slot_index < long_index, lengths, 0)
    after_long = jnp.where(slot_index > long_index, lengths, 0)
    long_length = LEN - jnp.sum(before, axis=1, keepdims=True) - jnp.sum(after_long, axis=1, keepdims=True)
    doc_sizes = jnp.where(slot_index == long_index, long_length, lengths)
    doc_ends = jnp.cumsum(doc_sizes, axis=1)
    return (doc_ends - doc_sizes).astype(jnp.int32)


def draw_left_stat(key, part):
    key = jax.random.fold_in(key, 21)
    return dominant(key, NBLK, BL, block_scale(BC))


def draw_right_stat(key, part):
    key = jax.random.fold_in(key, 22)
    return dominant(key, NBLK, BC, block_scale(BL))


def draw_left_root(key, part):
    key = jax.random.fold_in(key, 23)
    return dominant(key, NBLK, BL, jnp.ones((NBLK,), jnp.float32))


def draw_right_root(key, part):
    key = jax.random.fold_in(key, 24)
    return dominant(key, NBLK, BC, jnp.ones((NBLK,), jnp.float32))


def steps_of(rng, shape, split, low, top_value):
    factor_of = 1.0
    for dim, blocks in split:
        heights = jax.random.uniform(jax.random.fold_in(jax.random.fold_in(rng, 6), dim), (blocks,), jnp.float32, low / len(split), top_value / len(split))
        factor_of = factor_of * jnp.repeat(jnp.exp(heights), shape[dim] // blocks).reshape((-1,) + (1,) * (len(shape) - 1 - dim))
    return factor_of


def scatter_about(stream_key, shape, scale, bound, split=(), kind=jnp.bfloat16):
    factor_of = steps_of(stream_key, shape, split, -0.22, 0.18) if split else 1.0
    values = jax.random.normal(stream_key, shape, jnp.float32) * scale * factor_of
    return jnp.minimum(jnp.maximum(values, -bound), bound).astype(kind)


def setup_inputs(seed: int = 0) -> dict:
    keys = jax.random.split(jax.random.key(seed), 16)
    return {
        "tokens": scatter_about(keys[0], (ROWS, LEN, D), 1.0, 6.0, ((0, 4), (1, 8))),
        "cotangent": scatter_about(keys[1], (ROWS, LEN, D), 1.0, 6.0, ((0, 4), (1, 8))),
        "starts": draw_starts(jax.random.fold_in(keys[15], 71), 0),
        "gains": jnp.clip(1.0 + 0.1 * jax.random.normal(keys[3], (GLEN,), jnp.float32), 0.5, 1.5),
        "gain_moment": scatter_about(keys[4], (GLEN,), (TOKENS ** 0.5 / 9), 40.0, ((0, 32),), jnp.float32),
        "master_qa": scatter_about(keys[5], (D, QR), D ** -0.5, 0.125, ((0, 32),), jnp.float32),
        "master_qb": scatter_about(keys[6], (QR, HQ * HD), QR ** -0.5, 0.1875, ((0, 32),), jnp.float32),
        "master_kv": scatter_about(keys[7], (D, 2 * HD), D ** -0.5, 0.125, ((0, 32),), jnp.float32),
        "master_out": scatter_about(keys[8], (HQ * HD, D), (max(1, HQ * HD * 4 // LEN)) ** -0.5, 1.5, ((0, 32),), jnp.float32),
        "master_gu": scatter_about(keys[9], (D, 2 * FF), D ** -0.5, 0.125, ((0, 32),), jnp.float32),
        "master_down": scatter_about(keys[10], (FF, D), FF ** -0.5, 0.078125, ((0, 32),), jnp.float32),
        "left_stat": draw_left_stat(jax.random.fold_in(keys[15], 71), 0),
        "right_stat": draw_right_stat(jax.random.fold_in(keys[15], 71), 0),
        "left_root": draw_left_root(jax.random.fold_in(keys[15], 71), 0),
        "right_root": draw_right_root(jax.random.fold_in(keys[15], 71), 0),
    }


@jax.custom_vjp
def low(v):
    return lax.optimization_barrier(v.astype(jnp.bfloat16)).astype(jnp.float32)

@jax.custom_vjp
def low_back(v):
    return v

def low_keep(v):
    return (low(v), None)

def low_pass(kept, grad):
    return (grad,)

def back_keep(v):
    return (v, None)

def back_low(kept, grad):
    return (low(grad),)
low.defvjp(low_keep, low_pass)
low_back.defvjp(back_keep, back_low)
highest = lax.Precision.HIGHEST

def rms_norm(values, scaling):
    inverse = lax.rsqrt(lax.optimization_barrier(jnp.mean(values * values, axis=-1, keepdims=True)) + 1e-06)
    return values * inverse * scaling

def frequencies():
    half_dim = HD // 2
    return jnp.exp(jnp.arange(half_dim, dtype=jnp.float32) * (-2.0 * math.log(10000.0) / HD))

def rotate(values, cosine_table, sine_table):
    half_dim = values.shape[-1] // 2
    first_half = values[..., :half_dim]
    second_half = values[..., half_dim:]
    return jnp.concatenate([first_half * cosine_table - second_half * sine_table, second_half * cosine_table + first_half * sine_table], axis=-1)

def matmul(left_side, right_side):
    return jnp.dot(left_side, right_side, precision=highest, preferred_element_type=jnp.float32)

def layout(starts_row):
    places = jnp.arange(LEN, dtype=jnp.int32)
    inside = (starts_row[None, :] <= places[:, None]).astype(jnp.int32)
    document = (lax.optimization_barrier(jnp.sum(inside, axis=1)) - 1).astype(jnp.int32)
    picked = jnp.arange(NSEG, dtype=jnp.int32)[None, :] == document[:, None]
    first_place = lax.optimization_barrier(jnp.sum(jnp.where(picked, starts_row[None, :], 0), axis=1)).astype(jnp.int32)
    return (document, (places - first_place).astype(jnp.int32))

def attend_row(queries, key_rows, value_rows, document):
    query_block = min(512, LEN)
    indices = jnp.arange(LEN, dtype=jnp.int32)

    def one_block(number):
        begin_at = (number * query_block).astype(jnp.int32)
        row_queries = lax.dynamic_slice_in_dim(queries, begin_at, query_block, 0)
        row_doc = lax.dynamic_slice_in_dim(document, begin_at, query_block, 0)
        row_index = begin_at + jnp.arange(query_block, dtype=jnp.int32)
        allowed = (row_doc[:, None] == document[None, :]) & (row_index[:, None] >= indices[None, :])
        scores = jnp.einsum('qhd,kd->hqk', row_queries, key_rows, precision=highest) * HD ** (-0.5)
        scores = low_back(jnp.where(allowed[None], scores, -1e+30))
        row_top = lax.optimization_barrier(jnp.max(scores, axis=-1, keepdims=True))
        exponents = jnp.exp(scores - row_top)
        softmax_rows = low(exponents / lax.optimization_barrier(jnp.sum(exponents, axis=-1, keepdims=True)))
        return jnp.einsum('hqk,kd->qhd', softmax_rows, value_rows, precision=highest)
    outputs = lax.map(jax.checkpoint(one_block), jnp.arange(LEN // query_block, dtype=jnp.int32))
    return outputs.reshape(LEN, HQ * HD)

def forward(token_rows, gain_work, weight_qa, weight_qb, weight_kv, weight_out, weight_gu, weight_down, document, cosine_table, sine_table):
    gain_attn = gain_work[:D]
    gain_query = gain_work[D:D + QR]
    gain_mlp = gain_work[D + QR:]
    normed = low(rms_norm(token_rows, gain_attn))
    latent = low_back(matmul(normed, weight_qa))
    latent_norm = low(rms_norm(latent, gain_query))
    query_lin = low_back(matmul(latent_norm, weight_qb)).reshape(ROWS, LEN, HQ, HD)
    queries = low(rotate(query_lin, cosine_table[:, :, None, :], sine_table[:, :, None, :]))
    kv_lin = low_back(matmul(normed, weight_kv))
    key_rows = low(rotate(kv_lin[..., :HD], cosine_table, sine_table))
    value_rows = low(kv_lin[..., HD:])
    attended = lax.map(lambda members: attend_row(members[0], members[1], members[2], members[3]), (queries, key_rows, value_rows, document))
    attended = low_back(low(attended))
    branch = low_back(matmul(attended, weight_out))
    middle = token_rows + branch
    normed_mlp = low(rms_norm(middle, gain_mlp))
    gate_up = low_back(matmul(normed_mlp, weight_gu))
    hidden = low(jax.nn.silu(gate_up[..., :FF]) * gate_up[..., FF:])
    return middle + matmul(hidden, weight_down)

def to_blocks(matrices):
    pieces = [matrix.reshape(OWN, -1, BL, BC) for matrix in matrices]
    return jnp.concatenate(pieces, axis=1).reshape(NBLK, BL, BC)

def from_blocks(blocks, shapes):
    grouped = blocks.reshape(OWN, BPD, BL * BC)
    result = []
    offset = 0
    for shape_pair in shapes:
        block_count = shape_pair[0] * shape_pair[1] // (OWN * BL * BC)
        slab_piece = grouped[:, offset:offset + block_count, :]
        result.append(slab_piece.reshape(shape_pair[0], shape_pair[1]))
        offset = offset + block_count
    return result

def shampoo(grad_blocks, weight_blocks, left_stat, right_stat, left_root, right_root):
    left_new = 0.5 * left_stat + 0.5 * jnp.einsum('bij,bkj->bik', grad_blocks, grad_blocks, precision=highest)
    right_new = 0.5 * right_stat + 0.5 * jnp.einsum('bji,bjk->bik', grad_blocks, grad_blocks, precision=highest)
    direction = jnp.einsum('bij,bjk->bik', left_root, grad_blocks, precision=highest)
    direction = jnp.einsum('bij,bjk->bik', direction, right_root, precision=highest)
    weight_scale = jnp.sqrt(lax.optimization_barrier(jnp.mean(weight_blocks * weight_blocks, axis=(1, 2), keepdims=True)) + 1e-06)
    direction_scale = lax.rsqrt(lax.optimization_barrier(jnp.mean(direction * direction, axis=(1, 2), keepdims=True)) + 1e-06)
    return (weight_blocks - 0.3 * weight_scale * direction * direction_scale, left_new, right_new)

def reference(tokens, cotangent, starts, gains, gain_moment, master_qa, master_qb, master_kv, master_out, master_gu, master_down, left_stat, right_stat, left_root, right_root):
    document, places = jax.vmap(layout)(starts)
    angles = places.astype(jnp.float32)[..., None] * frequencies()[None, None, :]
    cosine_table = jnp.cos(angles)
    sine_table = jnp.sin(angles)
    masters = (master_qa, master_qb, master_kv, master_out, master_gu, master_down)
    working = [matrix.astype(jnp.bfloat16).astype(jnp.float32) for matrix in masters]
    gain_work = gains.astype(jnp.bfloat16).astype(jnp.float32)

    def layer_call(token_rows, gain_values, weight_qa, weight_qb, weight_kv, weight_out, weight_gu, weight_down):
        return forward(token_rows, gain_values, weight_qa, weight_qb, weight_kv, weight_out, weight_gu, weight_down, document, cosine_table, sine_table)
    output, pullback = jax.vjp(layer_call, tokens.astype(jnp.float32), gain_work, working[0], working[1], working[2], working[3], working[4], working[5])
    gradients = pullback(cotangent.astype(jnp.float32))
    grad_tokens = gradients[0]
    gain_grad = gradients[1]
    weight_grads = gradients[2:]
    shapes = [matrix.shape for matrix in masters]
    new_blocks, left_new, right_new = shampoo(to_blocks(weight_grads), to_blocks(masters), left_stat, right_stat, left_root, right_root)
    new_list = from_blocks(new_blocks, shapes)
    moment_new = 0.9 * gain_moment + 0.1 * gain_grad
    gains_new = gains - 0.4 / math.sqrt(TOKENS) * moment_new
    return (output.astype(jnp.bfloat16), grad_tokens, weight_grads[0], weight_grads[1], weight_grads[2], weight_grads[3], weight_grads[4], weight_grads[5], new_list[0], new_list[1], new_list[2], new_list[3], new_list[4], new_list[5], moment_new, gains_new, left_new, right_new)
```

```python
import functools
import math

import jax
import jax.numpy as jnp
import numpy as np
from jax import lax
from jax.experimental import pallas as pl
from jax.experimental.pallas import tpu as pltpu
from jax.sharding import PartitionSpec as P

D = 2048
QR = 1024
HQ = 16
HD = 256
FF = 5632
BL = 64
BC = 128
LANES = 128
GROUP = 8

bf16 = jnp.bfloat16
f32 = jnp.float32


def rms_norm(values, scaling):
    inverse = lax.rsqrt(jnp.mean(values * values, axis=-1, keepdims=True) + 1e-06)
    return values * inverse * scaling


def rms_back(values, scaling, grads):
    inverse = lax.rsqrt(jnp.mean(values * values, axis=-1, keepdims=True) + 1e-06)
    scaled = grads * scaling
    inner = jnp.mean(values * scaled, axis=-1, keepdims=True)
    d_values = inverse * scaled - values * (inverse * inverse * inverse * inner)
    d_scaling = jnp.sum(values * inverse * grads, axis=0)
    return d_values, d_scaling


def frequencies():
    half_dim = HD // 2
    return jnp.exp(jnp.arange(half_dim, dtype=f32) * (-2.0 * math.log(10000.0) / HD))


def rotate(values, cosine_table, sine_table):
    half_dim = values.shape[-1] // 2
    first_half = values[..., :half_dim]
    second_half = values[..., half_dim:]
    return jnp.concatenate(
        [
            first_half * cosine_table - second_half * sine_table,
            second_half * cosine_table + first_half * sine_table,
        ],
        axis=-1,
    )


def dot(left, right):
    return lax.dot_general(left, right, (((1,), (0,)), ((), ())), preferred_element_type=f32)


def dot_nt(left, right):
    return lax.dot_general(left, right, (((1,), (1,)), ((), ())), preferred_element_type=f32)


def dot_tn(left, right):
    return lax.dot_general(left, right, (((0,), (0,)), ((), ())), preferred_element_type=f32)


def after(value, *others):
    for other in others:
        entry = other[(0,) * other.ndim].astype(f32) * 0.0
        value = value + entry.astype(value.dtype)
    return value


def slot_order():
    order = np.zeros((2, 2, 2, 2), np.int32)
    for core in range(2):
        for a in range(2):
            for b in range(2):
                order[core, 0, a, b] = core + 2 * a + 4 * b
                order[core, 1, a, b] = core + 4 * a + 2 * b
    return order


class Layout:
    def __init__(self):
        self.n = lax.axis_size("seq")
        self.rows = lax.axis_size("row")
        self.outer = self.n // GROUP
        self.own = self.n * self.rows
        self.s = lax.axis_index("seq")
        self.r = lax.axis_index("row")
        self.i = self.s // self.outer
        self.u = self.s % self.outer

    def swap(self, values, bit):
        stride = self.outer << bit
        return lax.ppermute(values, "seq", [(s, s ^ stride) for s in range(self.n)])

    def swap_row(self, values, apart):
        return lax.ppermute(values, "row", [(r, r ^ apart) for r in range(self.rows)])

    def groups(self):
        return [[i * self.outer + u for i in range(GROUP)] for u in range(self.outer)]

    def outer_groups(self):
        return [[i * self.outer + u for u in range(self.outer)] for i in range(GROUP)]

    def gather(self, values, waits=()):
        t = values.shape[0] // 2
        first = values[:t]
        second = values[t:]
        first_near = self.swap(first, 2)
        second_near = self.swap(second, 1)
        first = jnp.concatenate([first, after(first_near, second_near, *waits)], axis=0)
        second = jnp.concatenate([second, after(second_near, first_near, *waits)], axis=0)
        first_far = self.swap(first, 1)
        second_far = self.swap(second, 2)
        both = jnp.concatenate(
            [first, after(first_far, second_far), second, after(second_far, first_far)], axis=0
        )
        return jnp.concatenate([both, self.swap(both, 0)], axis=0)

    def scatter(self, keep, send, waits=()):
        parts = after(keep + self.swap(send.astype(bf16), 0).astype(f32), *waits)
        q = parts.shape[0] // 4
        first_near = self.swap(parts[q : 2 * q].astype(bf16), 1)
        second_near = self.swap(parts[3 * q :].astype(bf16), 2)
        first = parts[:q] + after(first_near, second_near).astype(f32)
        second = parts[2 * q : 3 * q] + after(second_near, first_near).astype(f32)
        e = q // 2
        first = first[:e] + self.swap(first[e:].astype(bf16), 2).astype(f32)
        second = second[:e] + self.swap(second[e:].astype(bf16), 1).astype(f32)
        return jnp.concatenate([first, second], axis=0)

    def spread(self, values):
        t, c = values.shape
        stacked = values[None]
        for bit in (2, 1, 0):
            c = c // 2
            mine = (self.i >> bit) & 1
            keep = lax.dynamic_slice_in_dim(stacked, mine * c, c, stacked.ndim - 1)
            send = lax.dynamic_slice_in_dim(stacked, (1 - mine) * c, c, stacked.ndim - 1)
            stacked = jnp.concatenate([keep, self.swap(send, bit)], axis=0)
        stacked = stacked.reshape(2, 2, 2, 2, t // 2, c)
        halves = [stacked[:, :, :, 0], jnp.swapaxes(stacked[:, :, :, 1], 1, 2)]
        return jnp.stack(halves, axis=1).reshape(GROUP * t, c)

    def collect(self, values):
        t, c = values.shape
        t = t // GROUP
        stacked = values.reshape(2, 2, 2, 2, t // 2, c)
        halves = [stacked[:, 0], jnp.swapaxes(stacked[:, 1], 1, 2)]
        stacked = jnp.stack(halves, axis=3).reshape(GROUP * t, c)
        for bit in (0, 1, 2):
            rows = stacked.shape[0] // 2
            keep = stacked[:rows]
            other = self.swap(stacked[rows:], bit)
            high = ((self.i >> bit) & 1) == 1
            stacked = jnp.concatenate(
                [jnp.where(high, other, keep), jnp.where(high, keep, other)], axis=1
            )
        return stacked

    def scatter_dots(self, products, waits=()):
        def total(begin, end):
            return functools.reduce(
                jnp.add, [f(left[begin:end], right) for left, right, f in products]
            )

        half = products[0][0].shape[0] // 2
        send = total(half, 2 * half).astype(bf16)
        keep = total(0, half)
        return self.scatter(keep, send, waits)

    def own_rows(self, values):
        e = values.shape[0] // 16
        return jnp.concatenate([values[:e], values[4 * e : 5 * e]], axis=0)

    def gather_outer(self, values):
        if self.outer == 1:
            return values
        result = lax.all_gather(values, "seq", axis=0, axis_index_groups=self.outer_groups())
        return result.reshape((self.outer * self.rows,) + values.shape[1:])

    def gather_shard(self, values):
        flat = values.reshape(-1, values.shape[-1])
        flat = lax.all_gather(flat, "row", axis=0, tiled=True)
        return self.gather_outer(flat.reshape((self.rows,) + values.shape))

    def exchange(self, values):
        groups = None if self.outer == 1 else self.groups()
        return lax.all_to_all(values, "seq", 0, 0, axis_index_groups=groups)

    def sum_shard(self, values, *waits):
        if self.outer > 1:
            values = lax.psum_scatter(
                values.reshape(self.outer, -1, values.shape[-1]),
                "seq",
                scatter_dimension=0,
                axis_index_groups=self.outer_groups(),
                tiled=False,
            )
        values = lax.psum_scatter(values, "row", scatter_dimension=0, tiled=True)
        return after(values, *waits)

    def sum_all(self, values):
        for bit in range(self.n.bit_length() - 1):
            stride = 1 << bit
            values = values + lax.ppermute(values, "seq", [(s, s ^ stride) for s in range(self.n)])
        for bit in range(self.rows.bit_length() - 1):
            values = values + self.swap_row(values, 1 << bit)
        return values


def attention_forward(queries, keys_all, values_all, allowed):
    def one_head(head_queries):
        scores = dot_nt(head_queries, keys_all) * HD ** (-0.5)
        scores = jnp.where(allowed, scores, -1e30)
        row_top = jnp.max(scores, axis=-1, keepdims=True)
        exponents = jnp.exp(scores - row_top)
        totals = jnp.sum(exponents, axis=-1, keepdims=True)
        softmax_rows = (exponents / totals).astype(bf16)
        return dot(softmax_rows, values_all).astype(bf16), row_top + jnp.log(totals)

    pairs = [one_head(head_queries) for head_queries in queries]
    return [pair[0] for pair in pairs], [pair[1] for pair in pairs]


def attention_backward(queries, keys_all, values_all, allowed, log_totals, d_attended):
    d_keys = 0.0
    d_values = 0.0
    d_queries = []
    for head_queries, log_total, grads in zip(queries, log_totals, d_attended):
        scores = dot_nt(head_queries, keys_all) * HD ** (-0.5)
        softmax_rows = jnp.where(allowed, jnp.exp(jnp.where(allowed, scores - log_total, 0.0)), 0.0)
        d_probs = dot_nt(grads, values_all)
        row_delta = jnp.sum(softmax_rows * d_probs, axis=-1, keepdims=True)
        d_scores = (softmax_rows * (d_probs - row_delta)).astype(bf16)
        d_keys = d_keys + dot_tn(d_scores, head_queries) * HD ** (-0.5)
        d_values = d_values + dot_tn(softmax_rows.astype(bf16), grads)
        d_queries.append(dot(d_scores, keys_all) * HD ** (-0.5))
    return jnp.concatenate([d_keys, d_values], axis=1), d_queries


def column_chunks(parts, segments):
    width = parts[0].shape[1]
    piece = width // segments
    unit = LANES // 2
    if piece % LANES == 0:
        turned = parts
    else:
        turned = [pltpu.roll(part, unit, 1) for part in parts]
    lower = lax.broadcasted_iota(jnp.int32, (parts[0].shape[0], LANES), 1) < unit
    chunks = []
    for c in range(GROUP * width // LANES):
        found = []
        for half in range(2):
            segment, at = divmod(c * LANES + half * unit, GROUP * piece)
            member, at = divmod(at, piece)
            at = at + segment * piece
            if (at // unit) % 2 == half:
                found.append((False, member, at // LANES))
            else:
                found.append((True, member, ((at + unit) % width) // LANES))
        sides = [
            (turned if moved else parts)[member][:, k * LANES : (k + 1) * LANES]
            for moved, member, k in found
        ]
        chunks.append(sides[0] if found[0] == found[1] else jnp.where(lower, sides[0], sides[1]))
    return chunks


def shampoo_kernel(count, segments, g_ref, w_ref, lr_ref, rr_ref, ls_ref, rs_ref, *refs):
    grad_ref, new_ref, left_ref, right_ref, g_rows, w_rows = refs[-6:]
    height, width = w_ref.shape
    n = width // BC
    if segments:
        chunks = column_chunks([g_ref[i].astype(f32) for i in range(GROUP)], segments)
    else:
        chunks = [g_ref[:, c * BC : (c + 1) * BC].astype(f32) for c in range(n)]
    for c in range(n):
        columns = slice(c * BC, (c + 1) * BC)
        grad_ref[:, columns] = chunks[c]
        g_rows[pl.ds(c, height, stride=n), :] = chunks[c]
        w_rows[pl.ds(c, height, stride=n), :] = w_ref[:, columns]
    together = max(k for k in range(1, 12) if count % k == 0)

    def some_blocks(turn, carry):
        blocks = [turn * together + k for k in range(together)]
        rows = [pl.ds(pl.multiple_of(b * BL, BL), BL) for b in blocks]
        low = [g_rows[at, :].astype(bf16) for at in rows]
        step = [dot(lr_ref[b], x).astype(bf16) for b, x in zip(blocks, low)]
        left = [dot_nt(x, x) for x in low]
        step = [dot(x, rr_ref[b].astype(bf16)) for b, x in zip(blocks, step)]
        right = [dot_tn(x, x) for x in low]
        for b, x, y in zip(blocks, left, right):
            left_ref[b] = 0.5 * ls_ref[b] + 0.5 * x
            right_ref[b] = 0.5 * rs_ref[b] + 0.5 * y
        for at, x in zip(rows, step):
            weight = w_rows[at, :]
            weight_scale = jnp.sqrt(jnp.mean(weight * weight, keepdims=True) + 1e-06)
            step_scale = lax.rsqrt(jnp.mean(x * x, keepdims=True) + 1e-06)
            w_rows[at, :] = weight - (0.3 * weight_scale * step_scale) * x
        return carry

    lax.fori_loop(0, count // together, some_blocks, 0)
    for c in range(n):
        new_ref[:, c * BC : (c + 1) * BC] = w_rows[pl.ds(c, height, stride=n), :]


def shampoo(offset, grad, segments, weight, left_root, right_root, left_stat, right_stat, stats):
    m, width = weight.shape
    height = m
    for rows in (16, 32, 64):
        if m % rows == 0 and rows * width <= 16 * 11264 and (m // rows > 1 or height == m):
            height = rows
    count = height * width // (BL * BC)
    flat = pl.BlockSpec((height, width), lambda k: (k, 0))
    placed = lambda extent: pl.BlockSpec(
        (pl.Element(count), pl.Element(extent), pl.Element(extent)), lambda k: (k * count + offset, 0, 0)
    )
    if segments:
        given = pl.BlockSpec((GROUP, height, width // GROUP), lambda k: (0, k, 0))
    else:
        given = flat
    begun = [stat for stat in stats if stat is not None]
    blocks = m * width // (BL * BC)
    return pl.pallas_call(
        functools.partial(shampoo_kernel, count, segments),
        grid=(m // height,),
        in_specs=[given, flat, placed(BL), placed(BC), placed(BL), placed(BC)]
        + [pl.BlockSpec(memory_space=pltpu.MemorySpace.HBM)] * len(begun),
        out_specs=[flat, flat, placed(BL), placed(BC)],
        out_shape=[
            jax.ShapeDtypeStruct(weight.shape, f32),
            jax.ShapeDtypeStruct(weight.shape, f32),
            jax.ShapeDtypeStruct(left_stat.shape, f32),
            jax.ShapeDtypeStruct(right_stat.shape, f32),
        ],
        scratch_shapes=[pltpu.VMEM((height * width // BC, BC), f32)] * 2,
        input_output_aliases={6: 2, 7: 3} if begun else {},
        compiler_params=pltpu.CompilerParams(vmem_limit_bytes=48 * 1024 * 1024),
        cost_estimate=pl.CostEstimate(
            flops=blocks * 8 * BL * BC * BC,
            bytes_accessed=blocks * 4 * (3 * BC * BC + 3 * BL * BC + 3 * BL * BL),
            transcendentals=0,
        ),
        name="shampoo",
    )(grad, weight, left_root, right_root, left_stat, right_stat, *begun)


def on_device(
    tokens,
    cotangent,
    starts,
    gains,
    gain_moment,
    master_qa,
    master_qb,
    master_kv,
    master_out,
    master_gu,
    master_down,
    left_stat,
    right_stat,
    left_root,
    right_root,
):
    lay = Layout()
    tokens_here = tokens.shape[1]
    copies = lay.outer * lay.rows
    heads_here = HQ // GROUP
    hidden_here = FF // GROUP

    gains_here = gains.shape[0]
    def columns(matrix):
        m, width = matrix.shape
        return jnp.moveaxis(matrix.astype(bf16).reshape(m, GROUP, width // GROUP), 1, 0)

    def whole_shard(shard):
        return jnp.moveaxis(shard, 0, 1).reshape(-1, shard.shape[-1])

    query_parts = columns(master_qb)
    query_rows, query_width = query_parts.shape[1:]
    gain_row = jnp.pad(gains.astype(bf16), (0, query_width - gains_here))
    gain_row = jnp.broadcast_to(gain_row[None, None, :], (GROUP, 1, query_width))
    query_parts = lay.exchange(jnp.concatenate([query_parts, gain_row], axis=1))
    gain_group = query_parts[:, query_rows, :gains_here].reshape(1, -1)
    query_parts = query_parts[:, :query_rows]
    small_rows = master_qa.shape[0]
    small_width = QR + 2 * HD
    gain_group = jnp.pad(gain_group, ((0, 15), (0, small_width - gain_group.shape[1])))
    weight_small = jnp.concatenate([master_qa, master_kv], axis=1).astype(bf16)
    weight_small = lay.gather_shard(jnp.concatenate([weight_small, gain_group], axis=0))
    gain_values = weight_small[:, small_rows, : GROUP * gains_here]
    gain_values = jnp.moveaxis(gain_values.reshape(copies, GROUP, gains_here), 0, 1)
    gain_values = gain_values.reshape(-1).astype(f32)
    gain_attn = gain_values[:D]
    gain_query = gain_values[D : D + QR]
    gain_mlp = gain_values[D + QR :]
    weight_small = weight_small[:, :small_rows].reshape(-1, small_width)
    gate_up_parts = jnp.concatenate([columns(master_gu[:, :FF]), columns(master_gu[:, FF:])], axis=2)
    gate_up_parts = lay.exchange(after(gate_up_parts, query_parts))
    out_rows = master_out.shape[0]
    query_out = jnp.concatenate([query_parts.reshape(-1, D), master_out.astype(bf16)], axis=0)
    query_out = lay.gather_shard(after(query_out, weight_small))
    weight_out = query_out[:, -out_rows:].reshape(-1, D)
    split = gate_up_parts.shape[1] // 2
    gate_up_first = lay.gather_shard(after(gate_up_parts[:, :split], query_out))
    gate_up_second = lay.gather_shard(after(gate_up_parts[:, split:], gate_up_first))
    weight_gu = whole_shard(jnp.concatenate([gate_up_first, gate_up_second], axis=2))
    weight_qb = whole_shard(query_out[:, :-out_rows].reshape((copies,) + query_parts.shape))
    weight_down = lay.gather_shard(after(master_down.astype(bf16), gate_up_second)).reshape(-1, D)

    master_list = (master_qa, master_qb, master_kv, master_out, master_gu, master_down)
    left_root_low = lax.optimization_barrier(left_root.astype(bf16))
    left_stat_rows = lax.optimization_barrier(left_stat)

    half = tokens_here // 2
    order = slot_order()
    halves = np.broadcast_to(np.arange(2, dtype=np.int32)[None, :, None, None], order.shape)
    in_group = (
        (lay.i ^ jnp.asarray(order.reshape(-1, 1))) * (lay.outer * tokens_here)
        + jnp.asarray(halves.reshape(-1, 1)) * half
        + jnp.arange(half, dtype=jnp.int32)[None, :]
    ).reshape(-1)
    positions = in_group + lay.u * tokens_here
    key_positions = (
        jnp.arange(lay.outer, dtype=jnp.int32)[:, None] * tokens_here + in_group[None, :]
    ).reshape(-1)
    starts_row = starts[0]

    def document_of(places):
        return jnp.sum((starts_row[None, :] <= places[:, None]).astype(jnp.int32), axis=1) - 1

    document = document_of(positions)
    picked = jnp.arange(starts_row.shape[0], dtype=jnp.int32)[None, :] == document[:, None]
    place = positions - jnp.sum(jnp.where(picked, starts_row[None, :], 0), axis=1)
    angles = place.astype(f32)[:, None] * frequencies()[None, :]
    cosine_table = jnp.cos(angles)
    sine_table = jnp.sin(angles)
    allowed = (document[:, None] == document_of(key_positions)[None, :]) & (
        positions[:, None] >= key_positions[None, :]
    )

    token_rows = tokens[0].astype(f32)
    own_cosine = lay.own_rows(cosine_table)
    own_sine = lay.own_rows(sine_table)
    normed = rms_norm(token_rows, gain_attn).astype(bf16)
    normed_part = lay.spread(after(normed, gate_up_parts))
    latent_kv = lay.scatter_dots(
        [(normed_part, weight_small, dot)], (query_out,)
    )
    latent = latent_kv[:, :QR]
    own_keys = rotate(latent_kv[:, QR : QR + HD], own_cosine, own_sine)
    own_low = jnp.concatenate(
        [rms_norm(latent, gain_query), own_keys, latent_kv[:, QR + HD :]], axis=1
    )
    all_low = lay.gather(own_low.astype(bf16), (gate_up_first,))
    latent_norm = all_low[:, :QR]
    keys_all = all_low[:, QR : QR + HD]
    values_all = all_low[:, QR + HD :]
    query_lin = after(dot(latent_norm, weight_qb), gate_up_second)
    queries = [
        rotate(query_lin[:, h * HD : (h + 1) * HD], cosine_table, sine_table).astype(bf16)
        for h in range(heads_here)
    ]
    if lay.outer > 1:
        kv_all = lax.all_gather(
            jnp.concatenate([keys_all, values_all], axis=1),
            "seq",
            axis=0,
            tiled=True,
            axis_index_groups=lay.outer_groups(),
        )
        keys_all = kv_all[:, :HD]
        values_all = kv_all[:, HD:]
    attended, log_totals = attention_forward(queries, keys_all, values_all, allowed)
    attended = jnp.concatenate(attended, axis=1)
    middle = token_rows + lay.scatter_dots([(attended, weight_out, dot)], (weight_down,))
    normed_mlp = lay.gather(rms_norm(middle, gain_mlp).astype(bf16))
    grad_rows = lay.gather(after(cotangent[0], all_low))
    gate_up = dot(normed_mlp, weight_gu)
    gate = gate_up[:, :hidden_here]
    up = gate_up[:, hidden_here:]
    sigmoid_gate = jax.nn.sigmoid(gate)
    hidden = (gate * sigmoid_gate * up).astype(bf16)

    def column_parts(grad):
        m = grad.shape[0] // (GROUP * copies)
        parts = jnp.moveaxis(grad.reshape(GROUP, copies, m, -1), 1, 0)
        return parts.reshape(-1, grad.shape[1])

    part_down = dot_tn(hidden, grad_rows).astype(bf16)
    d_hidden = dot_nt(grad_rows, weight_down)
    d_gate = d_hidden * up * sigmoid_gate * (1.0 + gate * (1.0 - sigmoid_gate))
    d_up = d_hidden * gate * sigmoid_gate
    d_gate_up = jnp.concatenate([d_gate.astype(bf16), d_up.astype(bf16)], axis=1)
    d_gate_up = after(d_gate_up, part_down)
    part_gu = column_parts(dot_tn(normed_mlp, d_gate_up).astype(bf16))
    sum_down = lay.sum_shard(part_down)
    d_normed_mlp = lay.scatter_dots([(d_gate_up, weight_gu, dot_nt)], (part_gu,))
    d_middle_part, d_gain_mlp = rms_back(middle, gain_mlp, d_normed_mlp)
    sum_gu = lay.sum_shard(part_gu)
    d_middle = cotangent[0].astype(f32) + d_middle_part
    d_branch = lay.gather(d_middle.astype(bf16), (sum_down,))
    sizes = [matrix.size // (BL * BC) for matrix in master_list]
    offsets = [sum(sizes[:k]) for k in range(len(sizes))]
    grad_list = [None] * 6
    new_list = [None] * 6
    stats = (None, None)

    def update(k, grad, segments, stats):
        grad_list[k], new_list[k], *stats = shampoo(
            offsets[k],
            grad,
            segments,
            master_list[k],
            left_root_low,
            right_root,
            left_stat_rows,
            right_stat,
            stats,
        )
        return stats

    stats = update(5, sum_down, 0, stats)
    output = middle + lay.scatter_dots([(after(hidden, d_branch), weight_down, dot)])
    d_attended = after(dot_nt(d_branch, weight_out), new_list[5]).astype(bf16)
    d_heads = [d_attended[:, h * HD : (h + 1) * HD] for h in range(heads_here)]
    d_kv, d_queries = attention_backward(
        queries, keys_all, values_all, allowed, log_totals, d_heads
    )
    if lay.outer > 1:
        d_kv = lax.psum_scatter(
            d_kv.reshape(lay.outer, -1, 2 * HD),
            "seq",
            scatter_dimension=0,
            axis_index_groups=lay.outer_groups(),
            tiled=False,
        )
    d_query_lin = jnp.concatenate(
        [rotate(d_query, cosine_table, -sine_table).astype(bf16) for d_query in d_queries], axis=1
    )
    rows = d_query_lin.shape[0] // 2
    send = jnp.concatenate([dot_nt(d_query_lin[rows:], weight_qb), d_kv[rows:]], axis=1)
    keep = jnp.concatenate([dot_nt(d_query_lin[:rows], weight_qb), d_kv[:rows]], axis=1)
    part_qb = column_parts(dot_tn(latent_norm, d_query_lin).astype(bf16)).reshape(copies, -1, D)
    part_out = dot_tn(attended, d_branch).astype(bf16).reshape(copies, -1, D)
    part_qb_out = jnp.concatenate([part_qb, part_out], axis=1).reshape(-1, D)
    sums = lay.scatter(keep, after(send, sum_gu, output), (part_qb_out,))
    d_latent, d_gain_query = rms_back(latent, gain_query, sums[:, :QR])
    d_keys = rotate(sums[:, QR : QR + HD], own_cosine, -own_sine)
    d_low = jnp.concatenate([d_latent, d_keys, sums[:, QR + HD :]], axis=1).astype(bf16)
    sum_qb_out = lay.sum_shard(part_qb_out)
    d_low_all = lay.gather(d_low, (sum_qb_out,))
    part_small = dot_tn(normed_part, d_low_all).astype(bf16)
    d_normed = lay.collect(dot_nt(d_low_all, weight_small).astype(bf16)).astype(f32)
    d_tokens_part, d_gain_attn = rms_back(token_rows, gain_attn, d_normed)
    grad_tokens = d_middle + d_tokens_part

    gain_grad = jnp.concatenate([d_gain_attn, d_gain_query, d_gain_mlp]).reshape(-1, LANES)
    gain_grad = lay.sum_all(gain_grad).reshape(-1)
    owner = lay.s * lay.rows + lay.r
    gain_grad = lax.dynamic_slice_in_dim(gain_grad, owner * gains_here, gains_here, 0)

    sum_small = lay.sum_shard(part_small)
    sum_qb = sum_qb_out[:-out_rows].reshape(GROUP, -1, HQ * HD // GROUP)
    parts_qb = lay.exchange(after(sum_qb, part_small))
    parts_gu = lay.exchange(after(sum_gu, part_small).reshape(GROUP, -1, sum_gu.shape[1]))
    stats = update(3, sum_qb_out[-out_rows:], 0, stats)
    stats = update(4, parts_gu, 2, stats)
    stats = update(1, parts_qb, 1, stats)
    stats = update(0, sum_small[:, :QR], 0, stats)
    left_new, right_new = update(2, sum_small[:, QR:], 0, stats)
    total_tokens = tokens_here * lay.own
    moment_new = 0.9 * gain_moment + 0.1 * gain_grad
    gains_new = gains - 0.4 / math.sqrt(total_tokens) * moment_new
    return (
        output[None].astype(bf16),
        grad_tokens[None],
        *grad_list,
        *new_list,
        moment_new,
        gains_new,
        left_new,
        right_new,
    )


def solution(mesh):
    owned = P(("seq", "row"), None)
    owned_blocks = P(("seq", "row"), None, None)
    placed = (P("row", "seq", None),) * 2
    vector = P(("seq", "row"))
    return jax.shard_map(
        on_device,
        mesh=mesh,
        in_specs=placed + (P("row", None), vector, vector) + (owned,) * 6 + (owned_blocks,) * 4,
        out_specs=placed + (owned,) * 12 + (vector, vector) + (owned_blocks,) * 2,
        check_vma=False,
    )
```

```python
import functools
import math

import jax
import jax.numpy as jnp
import numpy as np
from jax import lax
from jax.experimental import pallas as pl
from jax.experimental.pallas import tpu as pltpu
from jax.sharding import PartitionSpec as P

D = 2048
QR = 1024
HQ = 16
HD = 256
FF = 5632
BL = 64
BC = 128
LANES = 128
GROUP = 8

bf16 = jnp.bfloat16
f32 = jnp.float32


def rms_norm(values, scaling):
    inverse = lax.rsqrt(jnp.mean(values * values, axis=-1, keepdims=True) + 1e-06)
    return values * inverse * scaling


def rms_back(values, scaling, grads):
    inverse = lax.rsqrt(jnp.mean(values * values, axis=-1, keepdims=True) + 1e-06)
    scaled = grads * scaling
    inner = jnp.mean(values * scaled, axis=-1, keepdims=True)
    d_values = inverse * scaled - values * (inverse * inverse * inverse * inner)
    d_scaling = jnp.sum(values * inverse * grads, axis=0)
    return d_values, d_scaling


def frequencies():
    half_dim = HD // 2
    return jnp.exp(jnp.arange(half_dim, dtype=f32) * (-2.0 * math.log(10000.0) / HD))


def rotate(values, cosine_table, sine_table):
    half_dim = values.shape[-1] // 2
    first_half = values[..., :half_dim]
    second_half = values[..., half_dim:]
    return jnp.concatenate(
        [
            first_half * cosine_table - second_half * sine_table,
            second_half * cosine_table + first_half * sine_table,
        ],
        axis=-1,
    )


def dot(left, right):
    return lax.dot_general(left, right, (((1,), (0,)), ((), ())), preferred_element_type=f32)


def dot_nt(left, right):
    return lax.dot_general(left, right, (((1,), (1,)), ((), ())), preferred_element_type=f32)


def dot_tn(left, right):
    return lax.dot_general(left, right, (((0,), (0,)), ((), ())), preferred_element_type=f32)


def after(value, *others):
    for other in others:
        entry = other[(0,) * other.ndim].astype(f32) * 0.0
        value = value + entry.astype(value.dtype)
    return value


def slot_order():
    order = np.zeros((2, 2, 2, 2), np.int32)
    for core in range(2):
        for a in range(2):
            for b in range(2):
                order[core, 0, a, b] = core + 2 * a + 4 * b
                order[core, 1, a, b] = core + 4 * a + 2 * b
    return order


class Layout:
    def __init__(self):
        self.n = lax.axis_size("seq")
        self.rows = lax.axis_size("row")
        self.outer = self.n // GROUP
        self.own = self.n * self.rows
        self.s = lax.axis_index("seq")
        self.r = lax.axis_index("row")
        self.i = self.s // self.outer
        self.u = self.s % self.outer

    def swap(self, values, bit):
        stride = self.outer << bit
        return lax.ppermute(values, "seq", [(s, s ^ stride) for s in range(self.n)])

    def swap_row(self, values, apart):
        return lax.ppermute(values, "row", [(r, r ^ apart) for r in range(self.rows)])

    def groups(self):
        return [[i * self.outer + u for i in range(GROUP)] for u in range(self.outer)]

    def outer_groups(self):
        return [[i * self.outer + u for u in range(self.outer)] for i in range(GROUP)]

    def gather(self, values, waits=()):
        t = values.shape[0] // 2
        first = values[:t]
        second = values[t:]
        first_near = self.swap(first, 2)
        second_near = self.swap(second, 1)
        first = jnp.concatenate([first, after(first_near, second_near, *waits)], axis=0)
        second = jnp.concatenate([second, after(second_near, first_near, *waits)], axis=0)
        first_far = self.swap(first, 1)
        second_far = self.swap(second, 2)
        both = jnp.concatenate(
            [first, after(first_far, second_far), second, after(second_far, first_far)], axis=0
        )
        return jnp.concatenate([both, self.swap(both, 0)], axis=0)

    def scatter(self, keep, send, waits=()):
        parts = after(keep + self.swap(send.astype(bf16), 0).astype(f32), *waits)
        q = parts.shape[0] // 4
        first_near = self.swap(parts[q : 2 * q].astype(bf16), 1)
        second_near = self.swap(parts[3 * q :].astype(bf16), 2)
        first = parts[:q] + after(first_near, second_near).astype(f32)
        second = parts[2 * q : 3 * q] + after(second_near, first_near).astype(f32)
        e = q // 2
        first = first[:e] + self.swap(first[e:].astype(bf16), 2).astype(f32)
        second = second[:e] + self.swap(second[e:].astype(bf16), 1).astype(f32)
        return jnp.concatenate([first, second], axis=0)

    def spread(self, values):
        t, c = values.shape
        stacked = values[None]
        for bit in (2, 1, 0):
            c = c // 2
            mine = (self.i >> bit) & 1
            keep = lax.dynamic_slice_in_dim(stacked, mine * c, c, stacked.ndim - 1)
            send = lax.dynamic_slice_in_dim(stacked, (1 - mine) * c, c, stacked.ndim - 1)
            stacked = jnp.concatenate([keep, self.swap(send, bit)], axis=0)
        stacked = stacked.reshape(2, 2, 2, 2, t // 2, c)
        halves = [stacked[:, :, :, 0], jnp.swapaxes(stacked[:, :, :, 1], 1, 2)]
        return jnp.stack(halves, axis=1).reshape(GROUP * t, c)

    def collect(self, values):
        t, c = values.shape
        t = t // GROUP
        stacked = values.reshape(2, 2, 2, 2, t // 2, c)
        halves = [stacked[:, 0], jnp.swapaxes(stacked[:, 1], 1, 2)]
        stacked = jnp.stack(halves, axis=3).reshape(GROUP * t, c)
        for bit in (0, 1, 2):
            rows = stacked.shape[0] // 2
            keep = stacked[:rows]
            other = self.swap(stacked[rows:], bit)
            high = ((self.i >> bit) & 1) == 1
            stacked = jnp.concatenate(
                [jnp.where(high, other, keep), jnp.where(high, keep, other)], axis=1
            )
        return stacked

    def scatter_dots(self, products, waits=(), send_waits=()):
        def total(begin, end):
            return functools.reduce(
                jnp.add, [f(left[begin:end], right) for left, right, f in products]
            )

        half = products[0][0].shape[0] // 2
        send = after(total(half, 2 * half), *send_waits).astype(bf16)
        keep = total(0, half)
        return self.scatter(keep, send, waits)

    def own_rows(self, values):
        e = values.shape[0] // 16
        return jnp.concatenate([values[:e], values[4 * e : 5 * e]], axis=0)

    def gather_outer(self, values):
        if self.outer == 1:
            return values
        result = lax.all_gather(values, "seq", axis=0, axis_index_groups=self.outer_groups())
        return result.reshape((self.outer * self.rows,) + values.shape[1:])

    def gather_shard(self, values):
        flat = values.reshape(-1, values.shape[-1])
        flat = lax.all_gather(flat, "row", axis=0, tiled=True)
        return self.gather_outer(flat.reshape((self.rows,) + values.shape))

    def exchange(self, values):
        groups = None if self.outer == 1 else self.groups()
        return lax.all_to_all(values, "seq", 0, 0, axis_index_groups=groups)

    def sum_shard(self, values, *waits):
        if self.outer > 1:
            values = lax.psum_scatter(
                values.reshape(self.outer, -1, values.shape[-1]),
                "seq",
                scatter_dimension=0,
                axis_index_groups=self.outer_groups(),
                tiled=False,
            )
        values = lax.psum_scatter(values, "row", scatter_dimension=0, tiled=True)
        return after(values, *waits)


def attention_forward(queries, keys_all, values_all, allowed):
    def one_head(head_queries):
        scores = dot_nt(head_queries, keys_all) * HD ** (-0.5)
        scores = jnp.where(allowed, scores, -1e30)
        row_top = jnp.max(scores, axis=-1, keepdims=True)
        exponents = jnp.exp(scores - row_top)
        totals = jnp.sum(exponents, axis=-1, keepdims=True)
        softmax_rows = (exponents / totals).astype(bf16)
        return dot(softmax_rows, values_all).astype(bf16), row_top + jnp.log(totals)

    pairs = [one_head(head_queries) for head_queries in queries]
    return [pair[0] for pair in pairs], [pair[1] for pair in pairs]


def attention_backward(queries, keys_all, values_all, allowed, log_totals, d_attended):
    d_keys = 0.0
    d_values = 0.0
    d_queries = []
    for head_queries, log_total, grads in zip(queries, log_totals, d_attended):
        scores = dot_nt(head_queries, keys_all) * HD ** (-0.5)
        softmax_rows = jnp.where(allowed, jnp.exp(jnp.where(allowed, scores - log_total, 0.0)), 0.0)
        d_probs = dot_nt(grads, values_all)
        row_delta = jnp.sum(softmax_rows * d_probs, axis=-1, keepdims=True)
        d_scores = (softmax_rows * (d_probs - row_delta)).astype(bf16)
        d_keys = d_keys + dot_tn(d_scores, head_queries) * HD ** (-0.5)
        d_values = d_values + dot_tn(softmax_rows.astype(bf16), grads)
        d_queries.append(dot(d_scores, keys_all) * HD ** (-0.5))
    return jnp.concatenate([d_keys, d_values], axis=1), d_queries


def column_chunks(parts, segments):
    width = parts[0].shape[1]
    piece = width // segments
    unit = LANES // 2
    if piece % LANES == 0:
        turned = parts
    else:
        turned = [pltpu.roll(part, unit, 1) for part in parts]
    lower = lax.broadcasted_iota(jnp.int32, (parts[0].shape[0], LANES), 1) < unit
    chunks = []
    for c in range(GROUP * width // LANES):
        found = []
        for half in range(2):
            segment, at = divmod(c * LANES + half * unit, GROUP * piece)
            member, at = divmod(at, piece)
            at = at + segment * piece
            if (at // unit) % 2 == half:
                found.append((False, member, at // LANES))
            else:
                found.append((True, member, ((at + unit) % width) // LANES))
        sides = [
            (turned if moved else parts)[member][:, k * LANES : (k + 1) * LANES]
            for moved, member, k in found
        ]
        chunks.append(sides[0] if found[0] == found[1] else jnp.where(lower, sides[0], sides[1]))
    return chunks


def shampoo_kernel(count, segments, g_ref, w_ref, lr_ref, rr_ref, ls_ref, rs_ref, *refs):
    grad_ref, new_ref, left_ref, right_ref, g_rows, w_rows = refs[-6:]
    height, width = w_ref.shape
    n = width // BC
    if segments:
        chunks = column_chunks([g_ref[i].astype(f32) for i in range(GROUP)], segments)
    else:
        chunks = [g_ref[:, c * BC : (c + 1) * BC].astype(f32) for c in range(n)]
    for c in range(n):
        columns = slice(c * BC, (c + 1) * BC)
        grad_ref[:, columns] = chunks[c]
        g_rows[pl.ds(c, height, stride=n), :] = chunks[c]
        w_rows[pl.ds(c, height, stride=n), :] = w_ref[:, columns]
    together = max(k for k in range(1, 12) if count % k == 0)

    def some_blocks(turn, carry):
        blocks = [turn * together + k for k in range(together)]
        rows = [pl.ds(pl.multiple_of(b * BL, BL), BL) for b in blocks]
        low = [g_rows[at, :].astype(bf16) for at in rows]
        step = [dot(lr_ref[b], x).astype(bf16) for b, x in zip(blocks, low)]
        left = [dot_nt(x, x) for x in low]
        step = [dot(x, rr_ref[b].astype(bf16)) for b, x in zip(blocks, step)]
        right = [dot_tn(x, x) for x in low]
        for b, x, y in zip(blocks, left, right):
            left_ref[b] = 0.5 * ls_ref[b] + 0.5 * x
            right_ref[b] = 0.5 * rs_ref[b] + 0.5 * y
        for at, x in zip(rows, step):
            weight = w_rows[at, :]
            weight_scale = jnp.sqrt(jnp.mean(weight * weight, keepdims=True) + 1e-06)
            step_scale = lax.rsqrt(jnp.mean(x * x, keepdims=True) + 1e-06)
            w_rows[at, :] = weight - (0.3 * weight_scale * step_scale) * x
        return carry

    lax.fori_loop(0, count // together, some_blocks, 0)
    for c in range(n):
        new_ref[:, c * BC : (c + 1) * BC] = w_rows[pl.ds(c, height, stride=n), :]


def shampoo(offset, grad, segments, weight, left_root, right_root, left_stat, right_stat, stats):
    m, width = weight.shape
    height = m
    for rows in (16, 32, 64):
        if m % rows == 0 and rows * width <= 16 * 11264 and (m // rows > 1 or height == m):
            height = rows
    count = height * width // (BL * BC)
    flat = pl.BlockSpec((height, width), lambda k: (k, 0))
    placed = lambda extent: pl.BlockSpec(
        (pl.Element(count), pl.Element(extent), pl.Element(extent)), lambda k: (k * count + offset, 0, 0)
    )
    if segments:
        given = pl.BlockSpec((GROUP, height, width // GROUP), lambda k: (0, k, 0))
    else:
        given = flat
    begun = [stat for stat in stats if stat is not None]
    blocks = m * width // (BL * BC)
    return pl.pallas_call(
        functools.partial(shampoo_kernel, count, segments),
        grid=(m // height,),
        in_specs=[given, flat, placed(BL), placed(BC), placed(BL), placed(BC)]
        + [pl.BlockSpec(memory_space=pltpu.MemorySpace.HBM)] * len(begun),
        out_specs=[flat, flat, placed(BL), placed(BC)],
        out_shape=[
            jax.ShapeDtypeStruct(weight.shape, f32),
            jax.ShapeDtypeStruct(weight.shape, f32),
            jax.ShapeDtypeStruct(left_stat.shape, f32),
            jax.ShapeDtypeStruct(right_stat.shape, f32),
        ],
        scratch_shapes=[pltpu.VMEM((height * width // BC, BC), f32)] * 2,
        input_output_aliases={6: 2, 7: 3} if begun else {},
        compiler_params=pltpu.CompilerParams(vmem_limit_bytes=48 * 1024 * 1024),
        cost_estimate=pl.CostEstimate(
            flops=blocks * 8 * BL * BC * BC,
            bytes_accessed=blocks * 4 * (3 * BC * BC + 3 * BL * BC + 3 * BL * BL),
            transcendentals=0,
        ),
        name="shampoo",
    )(grad, weight, left_root, right_root, left_stat, right_stat, *begun)


def on_device(
    tokens,
    cotangent,
    starts,
    gains,
    gain_moment,
    master_qa,
    master_qb,
    master_kv,
    master_out,
    master_gu,
    master_down,
    left_stat,
    right_stat,
    left_root,
    right_root,
):
    lay = Layout()
    tokens_here = tokens.shape[1]
    copies = lay.outer * lay.rows
    heads_here = HQ // GROUP
    hidden_here = FF // GROUP

    gains_here = gains.shape[0]
    def columns(matrix):
        m, width = matrix.shape
        return jnp.moveaxis(matrix.astype(bf16).reshape(m, GROUP, width // GROUP), 1, 0)

    def whole_shard(shard):
        return jnp.moveaxis(shard, 0, 1).reshape(-1, shard.shape[-1])

    query_parts = columns(master_qb)
    query_rows, query_width = query_parts.shape[1:]
    gain_row = jnp.pad(gains.astype(bf16), (0, query_width - gains_here))
    gain_row = jnp.broadcast_to(gain_row[None, None, :], (GROUP, 1, query_width))
    query_parts = lay.exchange(jnp.concatenate([query_parts, gain_row], axis=1))
    gain_group = query_parts[:, query_rows, :gains_here].reshape(1, -1)
    query_parts = query_parts[:, :query_rows]
    small_rows = master_qa.shape[0]
    small_width = QR + 2 * HD
    gain_group = jnp.pad(gain_group, ((0, 15), (0, small_width - gain_group.shape[1])))
    weight_small = jnp.concatenate([master_qa, master_kv], axis=1).astype(bf16)
    weight_small = lay.gather_shard(jnp.concatenate([weight_small, gain_group], axis=0))
    gain_values = weight_small[:, small_rows, : GROUP * gains_here]
    gain_values = jnp.moveaxis(gain_values.reshape(copies, GROUP, gains_here), 0, 1)
    gain_values = gain_values.reshape(-1).astype(f32)
    gain_attn = gain_values[:D]
    gain_query = gain_values[D : D + QR]
    gain_mlp = gain_values[D + QR :]
    weight_small = weight_small[:, :small_rows].reshape(-1, small_width)
    gate_up_parts = jnp.concatenate([columns(master_gu[:, :FF]), columns(master_gu[:, FF:])], axis=2)
    gate_up_parts = lay.exchange(after(gate_up_parts, query_parts))
    out_rows = master_out.shape[0]
    query_out = jnp.concatenate([query_parts.reshape(-1, D), master_out.astype(bf16)], axis=0)
    query_out = lay.gather_shard(after(query_out, weight_small))
    weight_out = query_out[:, -out_rows:].reshape(-1, D)
    split = gate_up_parts.shape[1] // 2
    gate_up_first = lay.gather_shard(after(gate_up_parts[:, :split], query_out))
    gate_up_second = lay.gather_shard(after(gate_up_parts[:, split:], gate_up_first))
    weight_gu = whole_shard(jnp.concatenate([gate_up_first, gate_up_second], axis=2))
    weight_qb = whole_shard(query_out[:, :-out_rows].reshape((copies,) + query_parts.shape))
    weight_down = lay.gather_shard(after(master_down.astype(bf16), gate_up_second)).reshape(-1, D)

    master_list = (master_qa, master_qb, master_kv, master_out, master_gu, master_down)
    left_root_low = left_root.astype(bf16)

    half = tokens_here // 2
    order = slot_order()
    halves = np.broadcast_to(np.arange(2, dtype=np.int32)[None, :, None, None], order.shape)
    in_group = (
        (lay.i ^ jnp.asarray(order.reshape(-1, 1))) * (lay.outer * tokens_here)
        + jnp.asarray(halves.reshape(-1, 1)) * half
        + jnp.arange(half, dtype=jnp.int32)[None, :]
    ).reshape(-1)
    positions = in_group + lay.u * tokens_here
    key_positions = (
        jnp.arange(lay.outer, dtype=jnp.int32)[:, None] * tokens_here + in_group[None, :]
    ).reshape(-1)
    starts_row = starts[0]

    def document_of(places):
        return jnp.sum((starts_row[None, :] <= places[:, None]).astype(jnp.int32), axis=1) - 1

    document = document_of(positions)
    picked = jnp.arange(starts_row.shape[0], dtype=jnp.int32)[None, :] == document[:, None]
    place = positions - jnp.sum(jnp.where(picked, starts_row[None, :], 0), axis=1)
    angles = place.astype(f32)[:, None] * frequencies()[None, :]
    cosine_table = jnp.cos(angles)
    sine_table = jnp.sin(angles)
    allowed = (document[:, None] == document_of(key_positions)[None, :]) & (
        positions[:, None] >= key_positions[None, :]
    )

    token_rows = tokens[0].astype(f32)
    own_cosine = lay.own_rows(cosine_table)
    own_sine = lay.own_rows(sine_table)
    normed = rms_norm(token_rows, gain_attn).astype(bf16)
    normed_part = lay.spread(after(normed, gate_up_parts))
    latent_kv = lay.scatter_dots(
        [(normed_part, weight_small, dot)], (query_out,)
    )
    latent = latent_kv[:, :QR]
    own_keys = rotate(latent_kv[:, QR : QR + HD], own_cosine, own_sine)
    own_low = jnp.concatenate(
        [rms_norm(latent, gain_query), own_keys, latent_kv[:, QR + HD :]], axis=1
    )
    all_low = lay.gather(own_low.astype(bf16), (gate_up_first,))
    latent_norm = all_low[:, :QR]
    keys_all = all_low[:, QR : QR + HD]
    values_all = all_low[:, QR + HD :]
    query_lin = dot(latent_norm, weight_qb)
    queries = [
        rotate(query_lin[:, h * HD : (h + 1) * HD], cosine_table, sine_table).astype(bf16)
        for h in range(heads_here)
    ]
    if lay.outer > 1:
        kv_all = lax.all_gather(
            jnp.concatenate([keys_all, values_all], axis=1),
            "seq",
            axis=0,
            tiled=True,
            axis_index_groups=lay.outer_groups(),
        )
        keys_all = kv_all[:, :HD]
        values_all = kv_all[:, HD:]
    attended, log_totals = attention_forward(queries, keys_all, values_all, allowed)
    attended = jnp.concatenate(attended, axis=1)
    middle = token_rows + lay.scatter_dots([(attended, weight_out, dot)], (gate_up_second,))
    normed_mlp = lay.gather(rms_norm(middle, gain_mlp).astype(bf16), (weight_down,))
    grad_rows = lay.gather(after(cotangent[0], all_low))
    gate_up = dot(normed_mlp, weight_gu)
    gate = gate_up[:, :hidden_here]
    up = gate_up[:, hidden_here:]
    sigmoid_gate = jax.nn.sigmoid(gate)
    hidden = (gate * sigmoid_gate * up).astype(bf16)

    def column_parts(grad):
        m = grad.shape[0] // (GROUP * copies)
        parts = jnp.moveaxis(grad.reshape(GROUP, copies, m, -1), 1, 0)
        return parts.reshape(-1, grad.shape[1])

    part_down = dot_tn(hidden, grad_rows).astype(bf16)
    d_hidden = dot_nt(grad_rows, weight_down)
    d_gate = d_hidden * up * sigmoid_gate * (1.0 + gate * (1.0 - sigmoid_gate))
    d_up = d_hidden * gate * sigmoid_gate
    d_gate_up = jnp.concatenate([d_gate.astype(bf16), d_up.astype(bf16)], axis=1)
    part_gu = column_parts(dot_tn(normed_mlp, d_gate_up).astype(bf16))
    sum_down = lay.sum_shard(part_down)
    d_normed_mlp = lay.scatter_dots([(d_gate_up, weight_gu, dot_nt)], (part_gu,), (part_down,))
    d_middle_part, d_gain_mlp = rms_back(middle, gain_mlp, d_normed_mlp)
    sum_gu = lay.sum_shard(part_gu)
    d_middle = cotangent[0].astype(f32) + d_middle_part
    d_branch = lay.gather(d_middle.astype(bf16), (sum_down,))
    sizes = [matrix.size // (BL * BC) for matrix in master_list]
    offsets = [sum(sizes[:k]) for k in range(len(sizes))]
    grad_list = [None] * 6
    new_list = [None] * 6
    stats = (None, None)

    def update(k, grad, segments, stats):
        grad_list[k], new_list[k], *stats = shampoo(
            offsets[k],
            grad,
            segments,
            master_list[k],
            left_root_low,
            right_root,
            left_stat,
            right_stat,
            stats,
        )
        return stats

    stats = update(5, sum_down, 0, stats)
    d_attended = after(dot_nt(d_branch, weight_out), new_list[5]).astype(bf16)
    d_heads = [d_attended[:, h * HD : (h + 1) * HD] for h in range(heads_here)]
    d_kv, d_queries = attention_backward(
        queries, keys_all, values_all, allowed, log_totals, d_heads
    )
    if lay.outer > 1:
        d_kv = lax.psum_scatter(
            d_kv.reshape(lay.outer, -1, 2 * HD),
            "seq",
            scatter_dimension=0,
            axis_index_groups=lay.outer_groups(),
            tiled=False,
        )
    d_query_lin = jnp.concatenate(
        [rotate(d_query, cosine_table, -sine_table).astype(bf16) for d_query in d_queries], axis=1
    )
    rows = d_query_lin.shape[0] // 2
    send = jnp.concatenate([dot_nt(d_query_lin[rows:], weight_qb), d_kv[rows:]], axis=1)
    keep = jnp.concatenate([dot_nt(d_query_lin[:rows], weight_qb), d_kv[:rows]], axis=1)
    part_qb = column_parts(dot_tn(latent_norm, d_query_lin).astype(bf16)).reshape(copies, -1, D)
    part_out = dot_tn(attended, d_branch).astype(bf16).reshape(copies, -1, D)
    part_qb_out = jnp.concatenate([part_qb, part_out], axis=1).reshape(-1, D)
    sums = lay.scatter(keep, after(send, sum_gu), (part_qb_out,))
    d_latent, d_gain_query = rms_back(latent, gain_query, sums[:, :QR])
    d_keys = rotate(sums[:, QR : QR + HD], own_cosine, -own_sine)
    d_low = jnp.concatenate([d_latent, d_keys, sums[:, QR + HD :]], axis=1).astype(bf16)
    sum_qb_out = lay.sum_shard(part_qb_out)
    parts_gu = lay.exchange(sum_gu.reshape(GROUP, -1, sum_gu.shape[1]))
    stats = update(4, parts_gu, 2, stats)
    d_low_all = lay.gather(d_low, (sum_qb_out, new_list[4]))
    part_small = dot_tn(normed_part, d_low_all).astype(bf16)
    d_normed = lay.collect(dot_nt(d_low_all, weight_small).astype(bf16)).astype(f32)
    d_tokens_part, d_gain_attn = rms_back(token_rows, gain_attn, d_normed)
    grad_tokens = d_middle + d_tokens_part

    gain_grad = jnp.concatenate([d_gain_attn, d_gain_query, d_gain_mlp]).reshape(-1, LANES)
    gain_grad = jnp.pad(
        gain_grad.reshape(lay.own, gains_here), ((0, 0), (0, -gains_here % LANES))
    )
    gain_grad = lax.all_to_all(gain_grad, ("seq", "row"), 0, 0, tiled=True)
    gain_grad = jnp.sum(gain_grad, axis=0)[:gains_here]

    output = middle + lay.scatter_dots([(after(hidden, part_small), weight_down, dot)])
    sum_small = lay.sum_shard(part_small)
    sum_qb = sum_qb_out[:-out_rows].reshape(GROUP, -1, HQ * HD // GROUP)
    parts_qb = lay.exchange(after(sum_qb, part_small))
    stats = update(3, sum_qb_out[-out_rows:], 0, stats)
    stats = update(1, parts_qb, 1, stats)
    stats = update(0, sum_small[:, :QR], 0, stats)
    left_new, right_new = update(2, sum_small[:, QR:], 0, stats)
    total_tokens = tokens_here * lay.own
    moment_new = 0.9 * gain_moment + 0.1 * gain_grad
    gains_new = gains - 0.4 / math.sqrt(total_tokens) * moment_new
    return (
        output[None].astype(bf16),
        grad_tokens[None],
        *grad_list,
        *new_list,
        moment_new,
        gains_new,
        left_new,
        right_new,
    )


def solution(mesh):
    owned = P(("seq", "row"), None)
    owned_blocks = P(("seq", "row"), None, None)
    placed = (P("row", "seq", None),) * 2
    vector = P(("seq", "row"))
    return jax.shard_map(
        on_device,
        mesh=mesh,
        in_specs=placed + (P("row", None), vector, vector) + (owned,) * 6 + (owned_blocks,) * 4,
        out_specs=placed + (owned,) * 12 + (vector, vector) + (owned_blocks,) * 2,
        check_vma=False,
    )
```

```python
import functools
import math

import jax
import jax.numpy as jnp
import numpy as np
from jax import lax
from jax.experimental import pallas as pl
from jax.experimental.pallas import tpu as pltpu
from jax.sharding import PartitionSpec as P

D = 2048
QR = 1024
HQ = 16
HD = 256
FF = 5632
BL = 64
BC = 128
LANES = 128
GROUP = 8

bf16 = jnp.bfloat16
f32 = jnp.float32


def rms_norm(values, scaling):
    inverse = lax.rsqrt(jnp.mean(values * values, axis=-1, keepdims=True) + 1e-06)
    return values * inverse * scaling


def rms_back(values, scaling, grads):
    inverse = lax.rsqrt(jnp.mean(values * values, axis=-1, keepdims=True) + 1e-06)
    scaled = grads * scaling
    inner = jnp.mean(values * scaled, axis=-1, keepdims=True)
    d_values = inverse * scaled - values * (inverse * inverse * inverse * inner)
    d_scaling = jnp.sum(values * inverse * grads, axis=0)
    return d_values, d_scaling


def frequencies():
    half_dim = HD // 2
    return jnp.exp(jnp.arange(half_dim, dtype=f32) * (-2.0 * math.log(10000.0) / HD))


def rotate(values, cosine_table, sine_table):
    half_dim = values.shape[-1] // 2
    first_half = values[..., :half_dim]
    second_half = values[..., half_dim:]
    return jnp.concatenate(
        [
            first_half * cosine_table - second_half * sine_table,
            second_half * cosine_table + first_half * sine_table,
        ],
        axis=-1,
    )


def dot(left, right):
    return lax.dot_general(left, right, (((1,), (0,)), ((), ())), preferred_element_type=f32)


def dot_nt(left, right):
    return lax.dot_general(left, right, (((1,), (1,)), ((), ())), preferred_element_type=f32)


def dot_tn(left, right):
    return lax.dot_general(left, right, (((0,), (0,)), ((), ())), preferred_element_type=f32)


def after(value, *others):
    for other in others:
        entry = other[(0,) * other.ndim].astype(f32) * 0.0
        value = value + entry.astype(value.dtype)
    return value


def slot_order():
    order = np.zeros((2, 2, 2, 2), np.int32)
    for core in range(2):
        for a in range(2):
            for b in range(2):
                order[core, 0, a, b] = core + 2 * a + 4 * b
                order[core, 1, a, b] = core + 4 * a + 2 * b
    return order


class Layout:
    def __init__(self):
        self.n = lax.axis_size("seq")
        self.rows = lax.axis_size("row")
        self.outer = self.n // GROUP
        self.own = self.n * self.rows
        self.s = lax.axis_index("seq")
        self.r = lax.axis_index("row")
        self.i = self.s // self.outer
        self.u = self.s % self.outer

    def swap(self, values, bit):
        stride = self.outer << bit
        return lax.ppermute(values, "seq", [(s, s ^ stride) for s in range(self.n)])

    def swap_row(self, values, apart):
        return lax.ppermute(values, "row", [(r, r ^ apart) for r in range(self.rows)])

    def groups(self):
        return [[i * self.outer + u for i in range(GROUP)] for u in range(self.outer)]

    def outer_groups(self):
        return [[i * self.outer + u for u in range(self.outer)] for i in range(GROUP)]

    def gather(self, values, waits=()):
        t = values.shape[0] // 2
        first = values[:t]
        second = values[t:]
        first_near = self.swap(first, 2)
        second_near = self.swap(second, 1)
        first = jnp.concatenate([first, after(first_near, second_near, *waits)], axis=0)
        second = jnp.concatenate([second, after(second_near, first_near, *waits)], axis=0)
        first_far = self.swap(first, 1)
        second_far = self.swap(second, 2)
        both = jnp.concatenate(
            [first, after(first_far, second_far), second, after(second_far, first_far)], axis=0
        )
        return jnp.concatenate([both, self.swap(both, 0)], axis=0)

    def scatter(self, keep, send, waits=()):
        parts = after(keep + self.swap(send.astype(bf16), 0).astype(f32), *waits)
        q = parts.shape[0] // 4
        first_near = self.swap(parts[q : 2 * q].astype(bf16), 1)
        second_near = self.swap(parts[3 * q :].astype(bf16), 2)
        first = parts[:q] + after(first_near, second_near).astype(f32)
        second = parts[2 * q : 3 * q] + after(second_near, first_near).astype(f32)
        e = q // 2
        first = first[:e] + self.swap(first[e:].astype(bf16), 2).astype(f32)
        second = second[:e] + self.swap(second[e:].astype(bf16), 1).astype(f32)
        return jnp.concatenate([first, second], axis=0)

    def spread(self, values):
        t, c = values.shape
        stacked = values[None]
        for bit in (2, 1, 0):
            c = c // 2
            mine = (self.i >> bit) & 1
            keep = lax.dynamic_slice_in_dim(stacked, mine * c, c, stacked.ndim - 1)
            send = lax.dynamic_slice_in_dim(stacked, (1 - mine) * c, c, stacked.ndim - 1)
            stacked = jnp.concatenate([keep, self.swap(send, bit)], axis=0)
        stacked = stacked.reshape(2, 2, 2, 2, t // 2, c)
        halves = [stacked[:, :, :, 0], jnp.swapaxes(stacked[:, :, :, 1], 1, 2)]
        return jnp.stack(halves, axis=1).reshape(GROUP * t, c)

    def collect(self, values):
        t, c = values.shape
        t = t // GROUP
        stacked = values.reshape(2, 2, 2, 2, t // 2, c)
        halves = [stacked[:, 0], jnp.swapaxes(stacked[:, 1], 1, 2)]
        stacked = jnp.stack(halves, axis=3).reshape(GROUP * t, c)
        for bit in (0, 1, 2):
            rows = stacked.shape[0] // 2
            keep = stacked[:rows]
            other = self.swap(stacked[rows:], bit)
            high = ((self.i >> bit) & 1) == 1
            stacked = jnp.concatenate(
                [jnp.where(high, other, keep), jnp.where(high, keep, other)], axis=1
            )
        return stacked

    def scatter_dots(self, products, waits=(), send_waits=()):
        def total(begin, end):
            return functools.reduce(
                jnp.add, [f(left[begin:end], right) for left, right, f in products]
            )

        half = products[0][0].shape[0] // 2
        send = after(total(half, 2 * half), *send_waits).astype(bf16)
        keep = total(0, half)
        return self.scatter(keep, send, waits)

    def own_rows(self, values):
        e = values.shape[0] // 16
        return jnp.concatenate([values[:e], values[4 * e : 5 * e]], axis=0)

    def gather_outer(self, values):
        if self.outer == 1:
            return values
        result = lax.all_gather(values, "seq", axis=0, axis_index_groups=self.outer_groups())
        return result.reshape((self.outer * self.rows,) + values.shape[1:])

    def gather_shard(self, values):
        flat = values.reshape(-1, values.shape[-1])
        flat = lax.all_gather(flat, "row", axis=0, tiled=True)
        return self.gather_outer(flat.reshape((self.rows,) + values.shape))

    def exchange(self, values):
        groups = None if self.outer == 1 else self.groups()
        return lax.all_to_all(values, "seq", 0, 0, axis_index_groups=groups)

    def sum_shard(self, values, *waits):
        if self.outer > 1:
            values = lax.psum_scatter(
                values.reshape(self.outer, -1, values.shape[-1]),
                "seq",
                scatter_dimension=0,
                axis_index_groups=self.outer_groups(),
                tiled=False,
            )
        values = lax.psum_scatter(values, "row", scatter_dimension=0, tiled=True)
        return after(values, *waits)


def attention_forward(queries, keys_all, values_all, allowed):
    def one_head(head_queries):
        scores = dot_nt(head_queries, keys_all) * HD ** (-0.5)
        scores = jnp.where(allowed, scores, -1e30)
        row_top = jnp.max(scores, axis=-1, keepdims=True)
        exponents = jnp.exp(scores - row_top)
        totals = jnp.sum(exponents, axis=-1, keepdims=True)
        softmax_rows = (exponents / totals).astype(bf16)
        return dot(softmax_rows, values_all).astype(bf16), row_top + jnp.log(totals)

    pairs = [one_head(head_queries) for head_queries in queries]
    return [pair[0] for pair in pairs], [pair[1] for pair in pairs]


def attention_backward(queries, keys_all, values_all, allowed, log_totals, d_attended):
    d_keys = 0.0
    d_values = 0.0
    d_queries = []
    for head_queries, log_total, grads in zip(queries, log_totals, d_attended):
        scores = dot_nt(head_queries, keys_all) * HD ** (-0.5)
        softmax_rows = jnp.where(allowed, jnp.exp(jnp.where(allowed, scores - log_total, 0.0)), 0.0)
        d_probs = dot_nt(grads, values_all)
        row_delta = jnp.sum(softmax_rows * d_probs, axis=-1, keepdims=True)
        d_scores = (softmax_rows * (d_probs - row_delta)).astype(bf16)
        d_keys = d_keys + dot_tn(d_scores, head_queries) * HD ** (-0.5)
        d_values = d_values + dot_tn(softmax_rows.astype(bf16), grads)
        d_queries.append(dot(d_scores, keys_all) * HD ** (-0.5))
    return jnp.concatenate([d_keys, d_values], axis=1), d_queries


def column_chunks(parts, segments):
    width = parts[0].shape[1]
    piece = width // segments
    unit = LANES // 2
    if piece % LANES == 0:
        turned = parts
    else:
        turned = [pltpu.roll(part, unit, 1) for part in parts]
    lower = lax.broadcasted_iota(jnp.int32, (parts[0].shape[0], LANES), 1) < unit
    chunks = []
    for c in range(GROUP * width // LANES):
        found = []
        for half in range(2):
            segment, at = divmod(c * LANES + half * unit, GROUP * piece)
            member, at = divmod(at, piece)
            at = at + segment * piece
            if (at // unit) % 2 == half:
                found.append((False, member, at // LANES))
            else:
                found.append((True, member, ((at + unit) % width) // LANES))
        sides = [
            (turned if moved else parts)[member][:, k * LANES : (k + 1) * LANES]
            for moved, member, k in found
        ]
        chunks.append(sides[0] if found[0] == found[1] else jnp.where(lower, sides[0], sides[1]))
    return chunks


def shampoo_kernel(count, segments, g_ref, w_ref, lr_ref, rr_ref, ls_ref, rs_ref, *refs):
    grad_ref, new_ref, left_ref, right_ref, g_rows, w_rows = refs[-6:]
    height, width = w_ref.shape
    n = width // BC
    if segments:
        chunks = column_chunks([g_ref[i].astype(f32) for i in range(GROUP)], segments)
    else:
        chunks = [g_ref[:, c * BC : (c + 1) * BC].astype(f32) for c in range(n)]
    for c in range(n):
        columns = slice(c * BC, (c + 1) * BC)
        grad_ref[:, columns] = chunks[c]
        g_rows[pl.ds(c, height, stride=n), :] = chunks[c]
        w_rows[pl.ds(c, height, stride=n), :] = w_ref[:, columns]
    together = max(k for k in range(1, 12) if count % k == 0)

    def some_blocks(turn, carry):
        blocks = [turn * together + k for k in range(together)]
        rows = [pl.ds(pl.multiple_of(b * BL, BL), BL) for b in blocks]
        low = [g_rows[at, :].astype(bf16) for at in rows]
        step = [dot(lr_ref[b], x).astype(bf16) for b, x in zip(blocks, low)]
        left = [dot_nt(x, x) for x in low]
        step = [dot(x, rr_ref[b].astype(bf16)) for b, x in zip(blocks, step)]
        right = [dot_tn(x, x) for x in low]
        for b, x, y in zip(blocks, left, right):
            left_ref[b] = 0.5 * ls_ref[b] + 0.5 * x
            right_ref[b] = 0.5 * rs_ref[b] + 0.5 * y
        for at, x in zip(rows, step):
            weight = w_rows[at, :]
            weight_scale = jnp.sqrt(jnp.mean(weight * weight, keepdims=True) + 1e-06)
            step_scale = lax.rsqrt(jnp.mean(x * x, keepdims=True) + 1e-06)
            w_rows[at, :] = weight - (0.3 * weight_scale * step_scale) * x
        return carry

    lax.fori_loop(0, count // together, some_blocks, 0)
    for c in range(n):
        new_ref[:, c * BC : (c + 1) * BC] = w_rows[pl.ds(c, height, stride=n), :]


def shampoo(offset, grad, segments, weight, left_root, right_root, left_stat, right_stat, stats):
    m, width = weight.shape
    height = m
    for rows in (16, 32, 64):
        if m % rows == 0 and rows * width <= 16 * 11264 and (m // rows > 1 or height == m):
            height = rows
    count = height * width // (BL * BC)
    flat = pl.BlockSpec((height, width), lambda k: (k, 0))
    placed = lambda extent: pl.BlockSpec(
        (pl.Element(count), pl.Element(extent), pl.Element(extent)), lambda k: (k * count + offset, 0, 0)
    )
    if segments:
        given = pl.BlockSpec((GROUP, height, width // GROUP), lambda k: (0, k, 0))
    else:
        given = flat
    begun = [stat for stat in stats if stat is not None]
    blocks = m * width // (BL * BC)
    return pl.pallas_call(
        functools.partial(shampoo_kernel, count, segments),
        grid=(m // height,),
        in_specs=[given, flat, placed(BL), placed(BC), placed(BL), placed(BC)]
        + [pl.BlockSpec(memory_space=pltpu.MemorySpace.HBM)] * len(begun),
        out_specs=[flat, flat, placed(BL), placed(BC)],
        out_shape=[
            jax.ShapeDtypeStruct(weight.shape, f32),
            jax.ShapeDtypeStruct(weight.shape, f32),
            jax.ShapeDtypeStruct(left_stat.shape, f32),
            jax.ShapeDtypeStruct(right_stat.shape, f32),
        ],
        scratch_shapes=[pltpu.VMEM((height * width // BC, BC), f32)] * 2,
        input_output_aliases={6: 2, 7: 3} if begun else {},
        compiler_params=pltpu.CompilerParams(vmem_limit_bytes=48 * 1024 * 1024),
        cost_estimate=pl.CostEstimate(
            flops=blocks * 8 * BL * BC * BC,
            bytes_accessed=blocks * 4 * (3 * BC * BC + 3 * BL * BC + 3 * BL * BL),
            transcendentals=0,
        ),
        name="shampoo",
    )(grad, weight, left_root, right_root, left_stat, right_stat, *begun)


def on_device(
    tokens,
    cotangent,
    starts,
    gains,
    gain_moment,
    master_qa,
    master_qb,
    master_kv,
    master_out,
    master_gu,
    master_down,
    left_stat,
    right_stat,
    left_root,
    right_root,
):
    lay = Layout()
    tokens_here = tokens.shape[1]
    copies = lay.outer * lay.rows
    heads_here = HQ // GROUP
    hidden_here = FF // GROUP

    gains_here = gains.shape[0]
    def columns(matrix):
        m, width = matrix.shape
        return jnp.moveaxis(matrix.astype(bf16).reshape(m, GROUP, width // GROUP), 1, 0)

    def whole_shard(shard):
        return jnp.moveaxis(shard, 0, 1).reshape(-1, shard.shape[-1])

    query_parts = columns(master_qb)
    query_rows, query_width = query_parts.shape[1:]
    gain_row = jnp.pad(gains.astype(bf16), (0, query_width - gains_here))
    gain_row = jnp.broadcast_to(gain_row[None, None, :], (GROUP, 1, query_width))
    query_parts = lay.exchange(jnp.concatenate([query_parts, gain_row], axis=1))
    gain_group = query_parts[:, query_rows, :gains_here].reshape(1, -1)
    query_parts = query_parts[:, :query_rows]
    small_rows = master_qa.shape[0]
    small_width = QR + 2 * HD
    gain_group = jnp.pad(gain_group, ((0, 15), (0, small_width - gain_group.shape[1])))
    weight_small = jnp.concatenate([master_qa, master_kv], axis=1).astype(bf16)
    weight_small = lay.gather_shard(jnp.concatenate([weight_small, gain_group], axis=0))
    gain_values = weight_small[:, small_rows, : GROUP * gains_here]
    gain_values = jnp.moveaxis(gain_values.reshape(copies, GROUP, gains_here), 0, 1)
    gain_values = gain_values.reshape(-1).astype(f32)
    gain_attn = gain_values[:D]
    gain_query = gain_values[D : D + QR]
    gain_mlp = gain_values[D + QR :]
    weight_small = weight_small[:, :small_rows].reshape(-1, small_width)
    gate_up_parts = jnp.concatenate([columns(master_gu[:, :FF]), columns(master_gu[:, FF:])], axis=2)
    gate_up_parts = lay.exchange(after(gate_up_parts, query_parts))
    out_rows = master_out.shape[0]
    query_out = jnp.concatenate([query_parts.reshape(-1, D), master_out.astype(bf16)], axis=0)
    query_out = lay.gather_shard(after(query_out, weight_small))
    weight_out = query_out[:, -out_rows:].reshape(-1, D)
    split = gate_up_parts.shape[1] * 3 // 4
    gate_up_first = lay.gather_shard(after(gate_up_parts[:, :split], query_out))
    gate_up_second = lay.gather_shard(after(gate_up_parts[:, split:], gate_up_first))
    weight_gu = whole_shard(jnp.concatenate([gate_up_first, gate_up_second], axis=2))
    weight_qb = whole_shard(query_out[:, :-out_rows].reshape((copies,) + query_parts.shape))
    weight_down = lay.gather_shard(after(master_down.astype(bf16), gate_up_second)).reshape(-1, D)

    master_list = (master_qa, master_qb, master_kv, master_out, master_gu, master_down)
    left_root_low = left_root.astype(bf16)

    half = tokens_here // 2
    order = slot_order()
    halves = np.broadcast_to(np.arange(2, dtype=np.int32)[None, :, None, None], order.shape)
    in_group = (
        (lay.i ^ jnp.asarray(order.reshape(-1, 1))) * (lay.outer * tokens_here)
        + jnp.asarray(halves.reshape(-1, 1)) * half
        + jnp.arange(half, dtype=jnp.int32)[None, :]
    ).reshape(-1)
    positions = in_group + lay.u * tokens_here
    key_positions = (
        jnp.arange(lay.outer, dtype=jnp.int32)[:, None] * tokens_here + in_group[None, :]
    ).reshape(-1)
    starts_row = starts[0]

    def document_of(places):
        return jnp.sum((starts_row[None, :] <= places[:, None]).astype(jnp.int32), axis=1) - 1

    document = document_of(positions)
    picked = jnp.arange(starts_row.shape[0], dtype=jnp.int32)[None, :] == document[:, None]
    place = positions - jnp.sum(jnp.where(picked, starts_row[None, :], 0), axis=1)
    angles = place.astype(f32)[:, None] * frequencies()[None, :]
    cosine_table = jnp.cos(angles)
    sine_table = jnp.sin(angles)
    allowed = (document[:, None] == document_of(key_positions)[None, :]) & (
        positions[:, None] >= key_positions[None, :]
    )

    token_rows = tokens[0].astype(f32)
    own_cosine = lay.own_rows(cosine_table)
    own_sine = lay.own_rows(sine_table)
    normed = rms_norm(token_rows, gain_attn).astype(bf16)
    normed_part = lay.spread(after(normed, gate_up_parts))
    latent_kv = lay.scatter_dots(
        [(normed_part, weight_small, dot)], (query_out,)
    )
    latent = latent_kv[:, :QR]
    own_keys = rotate(latent_kv[:, QR : QR + HD], own_cosine, own_sine)
    own_low = jnp.concatenate(
        [rms_norm(latent, gain_query), own_keys, latent_kv[:, QR + HD :]], axis=1
    )
    all_low = lay.gather(own_low.astype(bf16))
    latent_norm = all_low[:, :QR]
    keys_all = all_low[:, QR : QR + HD]
    values_all = all_low[:, QR + HD :]
    query_lin = after(dot(latent_norm, weight_qb), gate_up_first)
    queries = [
        rotate(query_lin[:, h * HD : (h + 1) * HD], cosine_table, sine_table).astype(bf16)
        for h in range(heads_here)
    ]
    if lay.outer > 1:
        kv_all = lax.all_gather(
            jnp.concatenate([keys_all, values_all], axis=1),
            "seq",
            axis=0,
            tiled=True,
            axis_index_groups=lay.outer_groups(),
        )
        keys_all = kv_all[:, :HD]
        values_all = kv_all[:, HD:]
    attended, log_totals = attention_forward(queries, keys_all, values_all, allowed)
    attended = jnp.concatenate(attended, axis=1)
    middle = token_rows + lay.scatter_dots([(attended, weight_out, dot)], (gate_up_second,))
    normed_mlp = lay.gather(rms_norm(middle, gain_mlp).astype(bf16), (weight_down,))
    grad_rows = lay.gather(after(cotangent[0], all_low))
    gate_up = dot(normed_mlp, weight_gu)
    gate = gate_up[:, :hidden_here]
    up = gate_up[:, hidden_here:]
    sigmoid_gate = jax.nn.sigmoid(gate)
    hidden = (gate * sigmoid_gate * up).astype(bf16)

    def column_parts(grad):
        m = grad.shape[0] // (GROUP * copies)
        parts = jnp.moveaxis(grad.reshape(GROUP, copies, m, -1), 1, 0)
        return parts.reshape(-1, grad.shape[1])

    part_down = dot_tn(hidden, grad_rows).astype(bf16)
    d_hidden = dot_nt(grad_rows, weight_down)
    d_gate = d_hidden * up * sigmoid_gate * (1.0 + gate * (1.0 - sigmoid_gate))
    d_up = d_hidden * gate * sigmoid_gate
    d_gate_up = jnp.concatenate([d_gate.astype(bf16), d_up.astype(bf16)], axis=1)
    part_gu = column_parts(dot_tn(normed_mlp, d_gate_up).astype(bf16))
    sum_down = lay.sum_shard(part_down)
    d_normed_mlp = lay.scatter_dots([(d_gate_up, weight_gu, dot_nt)], (part_gu,), (part_down,))
    d_middle_part, d_gain_mlp = rms_back(middle, gain_mlp, d_normed_mlp)
    sum_gu = lay.sum_shard(part_gu)
    d_middle = cotangent[0].astype(f32) + d_middle_part
    d_branch = lay.gather(d_middle.astype(bf16), (sum_down,))
    sizes = [matrix.size // (BL * BC) for matrix in master_list]
    offsets = [sum(sizes[:k]) for k in range(len(sizes))]
    grad_list = [None] * 6
    new_list = [None] * 6
    stats = (None, None)

    def update(k, grad, segments, stats):
        grad_list[k], new_list[k], *stats = shampoo(
            offsets[k],
            grad,
            segments,
            master_list[k],
            left_root_low,
            right_root,
            left_stat,
            right_stat,
            stats,
        )
        return stats

    stats = update(5, sum_down, 0, stats)
    d_attended = after(dot_nt(d_branch, weight_out), new_list[5]).astype(bf16)
    d_heads = [d_attended[:, h * HD : (h + 1) * HD] for h in range(heads_here)]
    d_kv, d_queries = attention_backward(
        queries, keys_all, values_all, allowed, log_totals, d_heads
    )
    if lay.outer > 1:
        d_kv = lax.psum_scatter(
            d_kv.reshape(lay.outer, -1, 2 * HD),
            "seq",
            scatter_dimension=0,
            axis_index_groups=lay.outer_groups(),
            tiled=False,
        )
    d_query_lin = jnp.concatenate(
        [rotate(d_query, cosine_table, -sine_table).astype(bf16) for d_query in d_queries], axis=1
    )
    rows = d_query_lin.shape[0] // 2
    send = jnp.concatenate([dot_nt(d_query_lin[rows:], weight_qb), d_kv[rows:]], axis=1)
    keep = jnp.concatenate([dot_nt(d_query_lin[:rows], weight_qb), d_kv[:rows]], axis=1)
    part_qb = column_parts(dot_tn(latent_norm, d_query_lin).astype(bf16)).reshape(copies, -1, D)
    part_out = dot_tn(attended, d_branch).astype(bf16).reshape(copies, -1, D)
    part_qb_out = jnp.concatenate([part_qb, part_out], axis=1).reshape(-1, D)
    sums = lay.scatter(keep, after(send, sum_gu), (part_qb_out,))
    d_latent, d_gain_query = rms_back(latent, gain_query, sums[:, :QR])
    d_keys = rotate(sums[:, QR : QR + HD], own_cosine, -own_sine)
    d_low = jnp.concatenate([d_latent, d_keys, sums[:, QR + HD :]], axis=1).astype(bf16)
    sum_qb_out = lay.sum_shard(part_qb_out)
    parts_gu = lay.exchange(sum_gu.reshape(GROUP, -1, sum_gu.shape[1]))
    stats = update(4, parts_gu, 2, stats)
    d_low_all = lay.gather(d_low, (sum_qb_out, new_list[4]))
    part_small = dot_tn(normed_part, d_low_all).astype(bf16)
    d_normed = lay.collect(dot_nt(d_low_all, weight_small).astype(bf16)).astype(f32)
    d_tokens_part, d_gain_attn = rms_back(token_rows, gain_attn, d_normed)
    grad_tokens = d_middle + d_tokens_part

    gain_grad = jnp.concatenate([d_gain_attn, d_gain_query, d_gain_mlp]).reshape(-1, LANES)
    gain_grad = jnp.pad(
        gain_grad.reshape(lay.own, gains_here), ((0, 0), (0, -gains_here % LANES))
    )
    gain_grad = lax.all_to_all(gain_grad, ("seq", "row"), 0, 0, tiled=True)
    gain_grad = jnp.sum(gain_grad, axis=0)[:gains_here]

    output = middle + lay.scatter_dots([(after(hidden, sums), weight_down, dot)])
    sum_small = lay.sum_shard(part_small)
    sum_qb = sum_qb_out[:-out_rows].reshape(GROUP, -1, HQ * HD // GROUP)
    parts_qb = lay.exchange(after(sum_qb, part_small))
    stats = update(3, sum_qb_out[-out_rows:], 0, stats)
    stats = update(1, parts_qb, 1, stats)
    stats = update(0, sum_small[:, :QR], 0, stats)
    left_new, right_new = update(2, sum_small[:, QR:], 0, stats)
    total_tokens = tokens_here * lay.own
    moment_new = 0.9 * gain_moment + 0.1 * gain_grad
    gains_new = gains - 0.4 / math.sqrt(total_tokens) * moment_new
    return (
        output[None].astype(bf16),
        grad_tokens[None],
        *grad_list,
        *new_list,
        moment_new,
        gains_new,
        left_new,
        right_new,
    )


def solution(mesh):
    owned = P(("seq", "row"), None)
    owned_blocks = P(("seq", "row"), None, None)
    placed = (P("row", "seq", None),) * 2
    vector = P(("seq", "row"))
    return jax.shard_map(
        on_device,
        mesh=mesh,
        in_specs=placed + (P("row", None), vector, vector) + (owned,) * 6 + (owned_blocks,) * 4,
        out_specs=placed + (owned,) * 12 + (vector, vector) + (owned_blocks,) * 2,
        check_vma=False,
    )
```
